512 devices in a mesh: dom: 64 (over y, x, core), col: 8 (over z).
Axes of the slice: x: 4, y: 8, z: 8, core: 2. Of those that a mesh axis runs over, the one named last changes fastest.
Arguments:
- matrix: float32 [1024, 8, 128, 128], P(('dom', 'col'))
- left_slots: int32 [1024, 8, 4], P(('dom', 'col')), may hold values from 0 to 3
- right_rows: int32 [1024, 8, 4], P(('dom', 'col')), may hold values from 0 to 1023, as said below
- right_slots: int32 [1024, 8, 4], P(('dom', 'col')), may hold values from 0 to 3
- pair_counts: int32 [1024, 8], P(('dom', 'col')), may hold values from 0 to 4
- diag_rows: int32 [1024, 4], P(('dom', 'col')), may hold values from 0 to 1023, as said below
Outputs:
- factors: float32 [1024, 8, 128, 128], P(('dom', 'col'))
The draws below stay inside these ranges and needn't reach their ends.
Inputs may be any that keep to these rules, and one draw needn't show every extreme that they name: With d the domain of row i at grid place (a, b): right_rows[i, s, p] is a row of domain d, or of the last 1 row of the domain at (a - 1, b) or (a, b - 1), or of the first 1 row of the domain at (a + 1, b) or (a, b + 1), where that domain exists. diag_rows[i, s] obeys the same rule as right_rows.
All inputs are finite; a program needn't handle non-finite values.
Results may differ from the reference program's by a relative error of at most 0.0003.
Values sent between devices are 32-bit elements; how exact they have to be, the bound alone decides.
A program may use at most 64 MiB of HBM per device.

```python
import jax
import jax.numpy as jnp
from jax import lax

BLOCK_DIM = 128
SLOT_COUNT = 8
LOWER_SLOTS = 4
UPPER_SLOTS = 4
PAIR_COUNT = 4
NEWTON_STEPS = 4
SWEEP_COUNT = 2
ROWS_DEV = 2
TOTAL_ROWS = 1024
N_DOM = 64
N_COL = 8


def window_rows(key, shape):
    rows = lax.broadcasted_iota(jnp.int32, shape, 0)
    domain = rows // ROWS_DEV
    first_place = domain // N_COL
    second_place = domain % N_COL
    half = ROWS_DEV // 2
    kind_key, own_key, rim_key = jax.random.split(key, 3)
    kind = jax.random.randint(kind_key, shape, 0, 5, dtype=jnp.int32)
    own_offset = jax.random.randint(own_key, shape, 0, ROWS_DEV, dtype=jnp.int32)
    rim_offset = jax.random.randint(rim_key, shape, 0, half, dtype=jnp.int32)
    own_row = domain * ROWS_DEV + own_offset
    before_first = (domain - N_COL) * ROWS_DEV + half + rim_offset
    after_first = (domain + N_COL) * ROWS_DEV + rim_offset
    before_second = (domain - 1) * ROWS_DEV + half + rim_offset
    after_second = (domain + 1) * ROWS_DEV + rim_offset
    chosen = jnp.where((kind == 1) & (first_place > 0), before_first, own_row)
    chosen = jnp.where((kind == 2) & (first_place < N_DOM - 1), after_first, chosen)
    chosen = jnp.where((kind == 3) & (second_place > 0), before_second, chosen)
    chosen = jnp.where((kind == 4) & (second_place < N_COL - 1), after_second, chosen)
    return chosen.astype(jnp.int32)


def draw_right_rows(key, part):
    key = jax.random.fold_in(key, 5)
    return window_rows(key, (TOTAL_ROWS, SLOT_COUNT, PAIR_COUNT))


def draw_diag_rows(key, part):
    key = jax.random.fold_in(key, 7)
    return window_rows(key, (TOTAL_ROWS, LOWER_SLOTS))


def draw_matrix(key, part):
    key = jax.random.fold_in(key, 11)
    first_key, second_key = jax.random.split(key)
    shape = (TOTAL_ROWS, SLOT_COUNT, BLOCK_DIM, BLOCK_DIM)
    noise = jax.random.normal(first_key, shape, jnp.float32)
    widest = 0.69
    scales = jnp.exp(jax.random.uniform(second_key, (TOTAL_ROWS, SLOT_COUNT, BLOCK_DIM, 1), jnp.float32, 0.0, widest))
    slot_ids = lax.broadcasted_iota(jnp.int32, shape, 1)
    row_ids = lax.broadcasted_iota(jnp.int32, shape, 2)
    column_ids = lax.broadcasted_iota(jnp.int32, shape, 3)
    identity = (row_ids == column_ids).astype(jnp.float32)
    diagonal_block = scales * (identity + 0.006 * noise)
    return jnp.where(slot_ids == LOWER_SLOTS, diagonal_block, 0.01 * noise)


def with_ends(drawn, stream_key, low, largest):
    longest = drawn.shape.index(max(drawn.shape))
    spots = []
    for shift in (0, 1):
        where = [jax.random.randint(jax.random.fold_in(stream_key, axis), (), 0, length) for axis, length in enumerate(drawn.shape)]
        where[longest] = (where[longest] + shift) % drawn.shape[longest]
        spots.append(tuple(where))
    return drawn.at[spots[0]].set(low).at[spots[1]].set(largest)


def setup_inputs(seed: int = 0) -> dict:
    keys = jax.random.split(jax.random.key(seed), 7)
    matrix = draw_matrix(jax.random.fold_in(keys[6], 71), 0)
    left_slots = with_ends(jax.random.randint(keys[1], (TOTAL_ROWS, SLOT_COUNT, PAIR_COUNT), 0, LOWER_SLOTS), jax.random.fold_in(keys[1], 1), 0, LOWER_SLOTS - 1).astype(jnp.int32)
    right_rows = draw_right_rows(jax.random.fold_in(keys[6], 71), 0)
    right_slots = with_ends(jax.random.randint(keys[3], (TOTAL_ROWS, SLOT_COUNT, PAIR_COUNT), 0, UPPER_SLOTS), jax.random.fold_in(keys[3], 1), 0, UPPER_SLOTS - 1).astype(jnp.int32)
    pair_counts = with_ends(jax.random.randint(keys[4], (TOTAL_ROWS, SLOT_COUNT), 0, PAIR_COUNT + 1), jax.random.fold_in(keys[4], 1), 0, PAIR_COUNT).astype(jnp.int32)
    diag_rows = draw_diag_rows(jax.random.fold_in(keys[6], 71), 0)
    return dict(matrix=matrix, left_slots=left_slots, right_rows=right_rows, right_slots=right_slots, pair_counts=pair_counts, diag_rows=diag_rows)


def product(first, second):
    return jnp.matmul(first, second, precision=lax.Precision.HIGHEST)


def newton_inverse(square):
    size = square.shape[-1]
    identity = jnp.eye(size, dtype=jnp.float32)
    diagonal = jnp.sum(square * identity, axis=-1)
    approx = identity * (1.0 / diagonal)[..., None, :]
    for newton_index in range(NEWTON_STEPS):
        approx = product(approx, 2.0 * identity - product(square, approx))
    return approx


def reference(matrix, left_slots, right_rows, right_slots, pair_counts, diag_rows):
    factors = matrix
    row_ids = jnp.arange(TOTAL_ROWS, dtype=jnp.int32)
    for sweep_index in range(SWEEP_COUNT):
        previous = factors

        def one_row(inputs):
            row_index, matrix_row, slots_row, rows_row, uslots_row, counts_row, diag_row = inputs
            own_row = previous[row_index]
            residue = matrix_row
            for pair_index in range(PAIR_COUNT):
                left_blocks = own_row[slots_row[:, pair_index]]
                right_blocks = previous[rows_row[:, pair_index], LOWER_SLOTS + uslots_row[:, pair_index]]
                live = (pair_index < counts_row).astype(jnp.float32)[:, None, None]
                residue = residue - product(live * left_blocks, right_blocks)
            inverses = newton_inverse(previous[diag_row, LOWER_SLOTS])
            lower_part = product(residue[:LOWER_SLOTS], inverses)
            return jnp.concatenate([lower_part, residue[LOWER_SLOTS:]], axis=0)

        factors = lax.map(one_row, (row_ids, matrix, left_slots, right_rows, right_slots, pair_counts, diag_rows))
    return factors
```

```python
import functools

import jax
import jax.numpy as jnp
from jax import lax
from jax.experimental import pallas as pl
from jax.experimental.pallas import tpu as pltpu
from jax.sharding import PartitionSpec as P

LOWER = 4
UPPER = 4
SLOTS = 8
PAIRS = 4
ROWS = 2
BLOCK = 128
NEWTON_STEPS = 4
OWN, FIRST, SECOND = 0, 1, 2
WINDOW = 3 * UPPER * 2
LEFTS = ROWS * LOWER
MESH = pl.DeviceIdType.MESH
F32, BF16 = jnp.float32, jnp.bfloat16


def split(value):
    high = value.astype(BF16)
    return high, (value - high.astype(F32)).astype(BF16)


def as_left(value):
    high, low = split(value)
    return jnp.concatenate([high, low, high], axis=1)


def as_right(value):
    high, low = split(value)
    return jnp.concatenate([high, high, low], axis=0)


def product(left, right):
    return jnp.dot(left, right, preferred_element_type=F32)


def newton_inverses(squares):
    rows = lax.broadcasted_iota(jnp.int32, (BLOCK, BLOCK), 0)
    columns = lax.broadcasted_iota(jnp.int32, (BLOCK, BLOCK), 1)
    on_diagonal = rows == columns
    identity = jnp.where(on_diagonal, 1.0, 0.0).astype(F32)
    errors, approxes = [], []
    for square in squares:
        diagonal = jnp.where(on_diagonal, square, 0.0)
        error = identity - square * (1.0 / jnp.sum(diagonal, axis=0, keepdims=True))
        errors.append(error)
        approxes.append((identity + error) * (1.0 / jnp.sum(diagonal, axis=1, keepdims=True)))
    errors = [product(as_left(error), as_right(error)) for error in errors]
    for step in range(1, NEWTON_STEPS):
        for index, (error, approx) in enumerate(zip(errors, approxes)):
            right = as_right(error)
            if step < NEWTON_STEPS - 1:
                both = product(as_left(jnp.concatenate([approx, error], axis=0)), right)
                approxes[index] = approx + both[:BLOCK]
                errors[index] = both[BLOCK:]
            else:
                approxes[index] = approx + product(as_left(approx), right)
    return approxes


def kernel(
    matrix_ref, left_hbm, rows_hbm, slots_hbm, counts_hbm, diag_hbm, out_ref,
    left_ref, rows_ref, slots_ref, counts_ref, diag_ref,
    held, lower, upper, halo, products, inverses, places, diag_places,
    load_sem, table_sem, send_sem, recv_sem,
):
    dom, col = lax.axis_index("dom"), lax.axis_index("col")
    doms, cols = lax.axis_size("dom"), lax.axis_size("col")
    own_domain = dom * cols + col
    neighbours = {FIRST: [(dom + 1, col), (dom - 1, col)], SECOND: [(dom, col + 1), (dom, col - 1)]}
    exists = {FIRST: [dom < doms - 1, dom > 0], SECOND: [col < cols - 1, col > 0]}

    def transfer(sweep, kind, e, slot):
        source = matrix_ref.at[1 - e, LOWER + slot] if sweep == 0 else upper.at[1 - e, slot]
        return pltpu.make_async_remote_copy(
            src_ref=source,
            dst_ref=halo.at[sweep, kind - 1, slot, e],
            send_sem=send_sem.at[sweep, kind - 1, slot, e],
            recv_sem=recv_sem.at[sweep, kind - 1, slot, e],
            device_id=neighbours[kind][e],
            device_id_type=MESH,
        )

    def start(sweep, kind, e, slot):
        @pl.when(exists[kind][e])
        def _():
            transfer(sweep, kind, e, slot).start()

    barrier = pltpu.get_barrier_semaphore()
    arrivals = 0
    for kind in (SECOND, FIRST):
        for e in range(2):
            @pl.when(exists[kind][e])
            def _():
                pl.semaphore_signal(
                    barrier, inc=1, device_id=neighbours[kind][e], device_id_type=MESH
                )
            arrivals = arrivals + exists[kind][e].astype(jnp.int32)
    load = pltpu.make_async_copy(matrix_ref, held, load_sem)
    load.start()
    tables = [
        pltpu.make_async_copy(source, target, table_sem.at[index])
        for index, (source, target) in enumerate(
            [
                (left_hbm, left_ref), (rows_hbm, rows_ref), (slots_hbm, slots_ref),
                (counts_hbm, counts_ref), (diag_hbm, diag_ref),
            ]
        )
    ]
    for table in tables:
        table.start()
    pl.semaphore_wait(barrier, arrivals)

    @pl.loop(0, UPPER)
    def _(slot):
        for kind in (SECOND, FIRST):
            for e in range(2):
                start(0, kind, e, slot)

    for kind in (FIRST, SECOND):
        for e in range(2):
            @pl.when(jnp.logical_not(exists[kind][1 - e]))
            def _():
                for sweep in range(2):
                    for slot in range(UPPER):
                        halo[sweep, kind - 1, slot, e] = jnp.zeros((BLOCK, BLOCK), F32)

    for table in tables:
        table.wait()

    def place_of(row):
        shift = lax.shift_right_arithmetic(row, 1) - own_domain
        own = shift == 0
        kind = jnp.where(own, OWN, jnp.where(jnp.abs(shift) == cols, FIRST, SECOND))
        e = jnp.where(own, lax.bitwise_and(row, 1), jnp.where(shift < 0, 0, 1))
        return kind, e

    @pl.loop(0, ROWS * SLOTS)
    def _(target):
        row, slot = lax.div(target, SLOTS), lax.rem(target, SLOTS)
        count = counts_ref[row, slot]
        for pair in range(PAIRS):
            kind, e = place_of(rows_ref[row, pair, slot])
            window = (kind * UPPER + slots_ref[row, pair, slot]) * 2 + e
            place = window * LEFTS + row * LOWER + left_ref[row, pair, slot]
            places[target * PAIRS + pair] = jnp.where(pair < count, place, WINDOW * LEFTS)

    @pl.loop(0, LEFTS)
    def _(target):
        kind, e = place_of(diag_ref[lax.div(target, LOWER), lax.rem(target, LOWER)])
        diag_places[target] = kind * 2 + e

    products[WINDOW * LEFTS] = jnp.zeros((BLOCK, BLOCK), F32)
    load.wait()

    @pl.loop(0, LEFTS)
    def _(index):
        lower[pl.ds(pl.multiple_of(index * BLOCK, BLOCK), BLOCK)] = as_left(
            held[lax.div(index, LOWER), lax.rem(index, LOWER)]
        )

    def multiply(kind, slot, first, second):
        right = jnp.concatenate([as_right(first), as_right(second)], axis=1)
        both = product(lower[...], right).reshape(LEFTS, BLOCK, 2 * BLOCK)
        start = (kind * UPPER + slot) * 2 * LEFTS
        products[pl.ds(start, LEFTS)] = both[:, :, :BLOCK]
        products[pl.ds(start + LEFTS, LEFTS)] = both[:, :, BLOCK:]

    def multiply_halo(sweep, kind, slot):
        for e in range(2):
            @pl.when(exists[kind][1 - e])
            def _():
                transfer(sweep, kind, e, slot).wait_recv()
        multiply(kind, slot, halo[sweep, kind - 1, slot, 0], halo[sweep, kind - 1, slot, 1])

    def fill(sweep):
        def own(row, slot):
            return held[row, LOWER + slot] if sweep == 0 else upper[row, slot]

        for slot in range(UPPER):
            multiply(OWN, slot, own(0, slot), own(1, slot))

        multiply_halo(sweep, FIRST, 0)
        multiply_halo(sweep, SECOND, 0)
        squares = [own(0, 0), own(1, 0)]
        for kind in (FIRST, SECOND):
            squares += [halo[sweep, kind - 1, 0, e] for e in range(2)]
        for index, inverse in enumerate(newton_inverses(squares)):
            inverses[index] = as_right(inverse)

        for slot in range(1, UPPER):
            multiply_halo(sweep, FIRST, slot)
            multiply_halo(sweep, SECOND, slot)

    def residue(row, slot):
        target = (row * SLOTS + slot) * PAIRS
        terms = [products[places[target + pair]] for pair in range(PAIRS)]
        return held[row, slot] - ((terms[0] + terms[1]) + (terms[2] + terms[3]))

    def lower_block(index):
        row, slot = index // LOWER, index % LOWER
        return product(as_left(residue(row, slot)), inverses[diag_places[index]])

    fill(0)

    @pl.loop(0, UPPER)
    def _(slot):
        for row in range(ROWS):
            upper[row, slot] = residue(row, LOWER + slot)
            for kind in (SECOND, FIRST):
                start(1, kind, 1 - row, slot)

    for index in range(LEFTS):
        lower[pl.ds(index * BLOCK, BLOCK)] = as_left(lower_block(index))

    fill(1)

    @pl.loop(0, UPPER)
    def _(slot):
        for row in range(ROWS):
            out_ref[row, LOWER + slot] = residue(row, LOWER + slot)

    for index in range(LEFTS):
        out_ref[index // LOWER, index % LOWER] = lower_block(index)

    @pl.loop(0, UPPER)
    def _(slot):
        for sweep in range(2):
            for kind in (SECOND, FIRST):
                for e in range(2):
                    @pl.when(exists[kind][e])
                    def _():
                        transfer(sweep, kind, e, slot).wait_send()


def local(matrix, left_slots, right_rows, right_slots, pair_counts, diag_rows):
    operands = [matrix]
    operands += [jnp.swapaxes(table, 1, 2) for table in (left_slots, right_rows, right_slots)]
    operands += [pair_counts, diag_rows]
    return pl.pallas_call(
        kernel,
        out_shape=pltpu.VMEM(matrix.shape, F32),
        in_specs=[pl.BlockSpec(memory_space=pltpu.HBM)] * 6,
        out_specs=pl.BlockSpec(memory_space=pltpu.VMEM),
        scratch_shapes=[
            pltpu.SMEM((ROWS, PAIRS, SLOTS), jnp.int32),
            pltpu.SMEM((ROWS, PAIRS, SLOTS), jnp.int32),
            pltpu.SMEM((ROWS, PAIRS, SLOTS), jnp.int32),
            pltpu.SMEM((ROWS, SLOTS), jnp.int32),
            pltpu.SMEM((ROWS, LOWER), jnp.int32),
            pltpu.VMEM((ROWS, SLOTS, BLOCK, BLOCK), F32),
            pltpu.VMEM((LEFTS * BLOCK, 3 * BLOCK), BF16),
            pltpu.VMEM((ROWS, UPPER, BLOCK, BLOCK), F32),
            pltpu.VMEM((2, 2, UPPER, 2, BLOCK, BLOCK), F32),
            pltpu.VMEM((WINDOW * LEFTS + 1, BLOCK, BLOCK), F32),
            pltpu.VMEM((6, 3 * BLOCK, BLOCK), BF16),
            pltpu.SMEM((ROWS * SLOTS * PAIRS,), jnp.int32),
            pltpu.SMEM((LEFTS,), jnp.int32),
            pltpu.SemaphoreType.DMA,
            pltpu.SemaphoreType.DMA((5,)),
            pltpu.SemaphoreType.DMA((2, 2, UPPER, 2)),
            pltpu.SemaphoreType.DMA((2, 2, UPPER, 2)),
        ],
        compiler_params=pltpu.CompilerParams(
            collective_id=0, has_side_effects=True, vmem_limit_bytes=48 * 2**20
        ),
    )(*(pltpu.with_memory_space_constraint(operand, pltpu.HBM) for operand in operands))


def solution(mesh):
    split_rows = ("dom", "col")
    return jax.shard_map(
        local,
        mesh=mesh,
        in_specs=(
            P(split_rows, None, None, None),
            P(split_rows, None, None),
            P(split_rows, None, None),
            P(split_rows, None, None),
            P(split_rows, None),
            P(split_rows, None),
        ),
        out_specs=P(split_rows, None, None, None),
        check_vma=False,
    )
```

```python
import functools

import jax
import jax.numpy as jnp
from jax import lax
from jax.experimental import pallas as pl
from jax.experimental.pallas import tpu as pltpu
from jax.sharding import PartitionSpec as P

LOWER = 4
UPPER = 4
SLOTS = 8
PAIRS = 4
ROWS = 2
BLOCK = 128
NEWTON_STEPS = 4
OWN, FIRST, SECOND = 0, 1, 2
WINDOW = 3 * UPPER * 2
LEFTS = ROWS * LOWER
MESH = pl.DeviceIdType.MESH
F32, BF16 = jnp.float32, jnp.bfloat16


def split(value):
    high = value.astype(BF16)
    return high, (value - high.astype(F32)).astype(BF16)


def as_left(value):
    high, low = split(value)
    return jnp.concatenate([high, low, high], axis=1)


def as_right(value):
    high, low = split(value)
    return jnp.concatenate([high, high, low], axis=0)


def product(left, right):
    return jnp.dot(left, right, preferred_element_type=F32)


def newton_inverses(squares):
    rows = lax.broadcasted_iota(jnp.int32, (BLOCK, BLOCK), 0)
    columns = lax.broadcasted_iota(jnp.int32, (BLOCK, BLOCK), 1)
    on_diagonal = rows == columns
    identity = jnp.where(on_diagonal, 1.0, 0.0).astype(F32)
    errors, approxes = [], []
    for square in squares:
        diagonal = jnp.where(on_diagonal, square, 0.0)
        error = identity - square * (1.0 / jnp.sum(diagonal, axis=0, keepdims=True))
        errors.append(error)
        approxes.append((identity + error) * (1.0 / jnp.sum(diagonal, axis=1, keepdims=True)))
    errors = [product(as_left(error), as_right(error)) for error in errors]
    for step in range(1, NEWTON_STEPS):
        for index, (error, approx) in enumerate(zip(errors, approxes)):
            right = as_right(error)
            if step < NEWTON_STEPS - 1:
                both = product(as_left(jnp.concatenate([approx, error], axis=0)), right)
                approxes[index] = approx + both[:BLOCK]
                errors[index] = both[BLOCK:]
            else:
                approxes[index] = approx + product(as_left(approx), right)
    return approxes


def kernel(
    matrix_ref, left_hbm, rows_hbm, slots_hbm, counts_hbm, diag_hbm, out_ref,
    left_ref, rows_ref, slots_ref, counts_ref, diag_ref,
    held, lower, upper, halo, products, inverses, places, diag_places,
    load_sem, table_sem, send_sem, recv_sem,
):
    dom, col = lax.axis_index("dom"), lax.axis_index("col")
    doms, cols = lax.axis_size("dom"), lax.axis_size("col")
    own_domain = dom * cols + col
    neighbours = {FIRST: [(dom + 1, col), (dom - 1, col)], SECOND: [(dom, col + 1), (dom, col - 1)]}
    exists = {FIRST: [dom < doms - 1, dom > 0], SECOND: [col < cols - 1, col > 0]}

    def transfer(sweep, kind, e, slot):
        source = matrix_ref.at[1 - e, LOWER + slot] if sweep == 0 else upper.at[1 - e, slot]
        return pltpu.make_async_remote_copy(
            src_ref=source,
            dst_ref=halo.at[sweep, kind - 1, slot, e],
            send_sem=send_sem.at[sweep, kind - 1, slot, e],
            recv_sem=recv_sem.at[sweep, kind - 1, slot, e],
            device_id=neighbours[kind][e],
            device_id_type=MESH,
        )

    def start(sweep, kind, e, slot):
        @pl.when(exists[kind][e])
        def _():
            transfer(sweep, kind, e, slot).start()

    barrier = pltpu.get_barrier_semaphore()
    arrivals = 0
    for kind in (SECOND, FIRST):
        for e in range(2):
            @pl.when(exists[kind][e])
            def _():
                pl.semaphore_signal(
                    barrier, inc=1, device_id=neighbours[kind][e], device_id_type=MESH
                )
            arrivals = arrivals + exists[kind][e].astype(jnp.int32)
    load = pltpu.make_async_copy(matrix_ref, held, load_sem)
    load.start()
    tables = [
        pltpu.make_async_copy(source, target, table_sem.at[index])
        for index, (source, target) in enumerate(
            [
                (left_hbm, left_ref), (rows_hbm, rows_ref), (slots_hbm, slots_ref),
                (counts_hbm, counts_ref), (diag_hbm, diag_ref),
            ]
        )
    ]
    for table in tables:
        table.start()
    pl.semaphore_wait(barrier, arrivals)

    @pl.loop(0, UPPER)
    def _(slot):
        for kind in (SECOND, FIRST):
            for e in range(2):
                start(0, kind, e, slot)

    for kind in (FIRST, SECOND):
        for e in range(2):
            @pl.when(jnp.logical_not(exists[kind][1 - e]))
            def _():
                for sweep in range(2):
                    for slot in range(UPPER):
                        pltpu.make_async_copy(
                            matrix_ref.at[0, LOWER + slot],
                            halo.at[sweep, kind - 1, slot, e],
                            recv_sem.at[sweep, kind - 1, slot, e],
                        ).start()

    for table in tables:
        table.wait()

    def place_of(row):
        shift = lax.shift_right_arithmetic(row, 1) - own_domain
        own = shift == 0
        kind = jnp.where(own, OWN, jnp.where(jnp.abs(shift) == cols, FIRST, SECOND))
        e = jnp.where(own, lax.bitwise_and(row, 1), jnp.where(shift < 0, 0, 1))
        return kind, e

    @pl.loop(0, ROWS * SLOTS)
    def _(target):
        row, slot = lax.div(target, SLOTS), lax.rem(target, SLOTS)
        count = counts_ref[row, slot]
        for pair in range(PAIRS):
            kind, e = place_of(rows_ref[row, pair, slot])
            window = (kind * UPPER + slots_ref[row, pair, slot]) * 2 + e
            place = window * LEFTS + row * LOWER + left_ref[row, pair, slot]
            places[target * PAIRS + pair] = jnp.where(pair < count, place, WINDOW * LEFTS)

    @pl.loop(0, LEFTS)
    def _(target):
        kind, e = place_of(diag_ref[lax.div(target, LOWER), lax.rem(target, LOWER)])
        diag_places[target] = kind * 2 + e

    products[WINDOW * LEFTS] = jnp.zeros((BLOCK, BLOCK), F32)
    load.wait()

    @pl.loop(0, LEFTS)
    def _(index):
        lower[pl.ds(pl.multiple_of(index * BLOCK, BLOCK), BLOCK)] = as_left(
            held[lax.div(index, LOWER), lax.rem(index, LOWER)]
        )

    def multiply(kind, slot, first, second):
        right = jnp.concatenate([as_right(first), as_right(second)], axis=1)
        both = product(lower[...], right).reshape(LEFTS, BLOCK, 2 * BLOCK)
        start = (kind * UPPER + slot) * 2 * LEFTS
        products[pl.ds(start, LEFTS)] = both[:, :, :BLOCK]
        products[pl.ds(start + LEFTS, LEFTS)] = both[:, :, BLOCK:]

    def multiply_halo(sweep, *steps):
        for kind, slot in steps:
            for e in range(2):
                transfer(sweep, kind, e, slot).wait_recv()
        for kind, slot in steps:
            multiply(kind, slot, halo[sweep, kind - 1, slot, 0], halo[sweep, kind - 1, slot, 1])

    def wait_sent(sweep, slots):
        for slot in slots:
            for kind in (FIRST, SECOND):
                for e in range(2):
                    @pl.when(exists[kind][e])
                    def _():
                        transfer(sweep, kind, e, slot).wait_send()

    def fill(sweep):
        def own(row, slot):
            return held[row, LOWER + slot] if sweep == 0 else upper[row, slot]

        for slot in range(UPPER):
            multiply(OWN, slot, own(0, slot), own(1, slot))
        if sweep == 1:
            wait_sent(0, range(UPPER))
        multiply_halo(sweep, (FIRST, 0), (SECOND, 0))
        squares = [own(0, 0), own(1, 0)]
        for kind in (FIRST, SECOND):
            squares += [halo[sweep, kind - 1, 0, e] for e in range(2)]
        for index, inverse in enumerate(newton_inverses(squares)):
            inverses[index] = as_right(inverse)
        multiply_halo(sweep, (FIRST, 1), (FIRST, 2), (SECOND, 1))
        multiply_halo(sweep, (FIRST, 3), (SECOND, 2))
        if sweep == 1:
            wait_sent(1, range(UPPER - 1))
        multiply_halo(sweep, (SECOND, 3))

    def residue(row, slot):
        target = (row * SLOTS + slot) * PAIRS
        terms = [products[places[target + pair]] for pair in range(PAIRS)]
        return held[row, slot] - ((terms[0] + terms[1]) + (terms[2] + terms[3]))

    def lower_block(index):
        row, slot = index // LOWER, index % LOWER
        return product(as_left(residue(row, slot)), inverses[diag_places[index]])

    fill(0)
    for slots in ((0,), (1, 2, 3)):
        for slot in slots:
            for row in range(ROWS):
                upper[row, slot] = residue(row, LOWER + slot)
        for slot in slots:
            for kind in (SECOND, FIRST):
                for e in range(2):
                    start(1, kind, e, slot)
    for index in range(LEFTS):
        lower[pl.ds(index * BLOCK, BLOCK)] = as_left(lower_block(index))

    fill(1)
    for index in range(LEFTS):
        out_ref[index // LOWER, index % LOWER] = lower_block(index)
    for slot in range(UPPER):
        for row in range(ROWS):
            out_ref[row, LOWER + slot] = residue(row, LOWER + slot)
    wait_sent(1, (UPPER - 1,))


def local(matrix, left_slots, right_rows, right_slots, pair_counts, diag_rows):
    operands = [matrix]
    operands += [jnp.swapaxes(table, 1, 2) for table in (left_slots, right_rows, right_slots)]
    operands += [pair_counts, diag_rows]
    return pl.pallas_call(
        kernel,
        out_shape=pltpu.VMEM(matrix.shape, F32),
        in_specs=[pl.BlockSpec(memory_space=pltpu.HBM)] * 6,
        out_specs=pl.BlockSpec(memory_space=pltpu.VMEM),
        scratch_shapes=[
            pltpu.SMEM((ROWS, PAIRS, SLOTS), jnp.int32),
            pltpu.SMEM((ROWS, PAIRS, SLOTS), jnp.int32),
            pltpu.SMEM((ROWS, PAIRS, SLOTS), jnp.int32),
            pltpu.SMEM((ROWS, SLOTS), jnp.int32),
            pltpu.SMEM((ROWS, LOWER), jnp.int32),
            pltpu.VMEM((ROWS, SLOTS, BLOCK, BLOCK), F32),
            pltpu.VMEM((LEFTS * BLOCK, 3 * BLOCK), BF16),
            pltpu.VMEM((ROWS, UPPER, BLOCK, BLOCK), F32),
            pltpu.VMEM((2, 2, UPPER, 2, BLOCK, BLOCK), F32),
            pltpu.VMEM((WINDOW * LEFTS + 1, BLOCK, BLOCK), F32),
            pltpu.VMEM((6, 3 * BLOCK, BLOCK), BF16),
            pltpu.SMEM((ROWS * SLOTS * PAIRS,), jnp.int32),
            pltpu.SMEM((LEFTS,), jnp.int32),
            pltpu.SemaphoreType.DMA,
            pltpu.SemaphoreType.DMA((5,)),
            pltpu.SemaphoreType.DMA((2, 2, UPPER, 2)),
            pltpu.SemaphoreType.DMA((2, 2, UPPER, 2)),
        ],
        compiler_params=pltpu.CompilerParams(
            collective_id=0, has_side_effects=True, vmem_limit_bytes=48 * 2**20
        ),
    )(*(pltpu.with_memory_space_constraint(operand, pltpu.HBM) for operand in operands))


def solution(mesh):
    split_rows = ("dom", "col")
    return jax.shard_map(
        local,
        mesh=mesh,
        in_specs=(
            P(split_rows, None, None, None),
            P(split_rows, None, None),
            P(split_rows, None, None),
            P(split_rows, None, None),
            P(split_rows, None),
            P(split_rows, None),
        ),
        out_specs=P(split_rows, None, None, None),
        check_vma=False,
    )
```

```python
import functools

import jax
import jax.numpy as jnp
from jax import lax
from jax.experimental import pallas as pl
from jax.experimental.pallas import tpu as pltpu
from jax.sharding import PartitionSpec as P

LOWER = 4
UPPER = 4
SLOTS = 8
PAIRS = 4
ROWS = 2
BLOCK = 128
NEWTON_STEPS = 4
OWN, FIRST, SECOND = 0, 1, 2
WINDOW = 3 * UPPER * 2
LEFTS = ROWS * LOWER
MESH = pl.DeviceIdType.MESH
F32, BF16 = jnp.float32, jnp.bfloat16


def split(value):
    high = value.astype(BF16)
    return high, (value - high.astype(F32)).astype(BF16)


def as_left(value):
    high, low = split(value)
    return jnp.concatenate([high, low, high], axis=1)


def as_right(value):
    high, low = split(value)
    return jnp.concatenate([high, high, low], axis=0)


def product(left, right):
    return jnp.dot(left, right, preferred_element_type=F32)


def newton_inverses(squares):
    rows = lax.broadcasted_iota(jnp.int32, (BLOCK, BLOCK), 0)
    columns = lax.broadcasted_iota(jnp.int32, (BLOCK, BLOCK), 1)
    on_diagonal = rows == columns
    identity = jnp.where(on_diagonal, 1.0, 0.0).astype(F32)
    errors, approxes = [], []
    for square in squares:
        diagonal = jnp.where(on_diagonal, square, 0.0)
        error = identity - square * (1.0 / jnp.sum(diagonal, axis=0, keepdims=True))
        errors.append(error)
        approxes.append((identity + error) * (1.0 / jnp.sum(diagonal, axis=1, keepdims=True)))
    errors = [product(as_left(error), as_right(error)) for error in errors]
    for step in range(1, NEWTON_STEPS):
        for index, (error, approx) in enumerate(zip(errors, approxes)):
            right = as_right(error)
            if step < NEWTON_STEPS - 1:
                both = product(as_left(jnp.concatenate([approx, error], axis=0)), right)
                approxes[index] = approx + both[:BLOCK]
                errors[index] = both[BLOCK:]
            else:
                approxes[index] = approx + product(as_left(approx), right)
    return approxes


def kernel(
    matrix_ref, left_hbm, rows_hbm, slots_hbm, counts_hbm, diag_hbm, out_ref,
    left_ref, rows_ref, slots_ref, counts_ref, diag_ref,
    held, lower, rights, upper, halo, products, inverses, places, diag_places,
    load_sem, table_sem, send_sem, recv_sem,
):
    dom, col = lax.axis_index("dom"), lax.axis_index("col")
    doms, cols = lax.axis_size("dom"), lax.axis_size("col")
    own_domain = dom * cols + col
    neighbours = {FIRST: [(dom + 1, col), (dom - 1, col)], SECOND: [(dom, col + 1), (dom, col - 1)]}
    exists = {FIRST: [dom < doms - 1, dom > 0], SECOND: [col < cols - 1, col > 0]}

    def transfer(sweep, kind, e, slot):
        source = held.at[1 - e, LOWER + slot] if sweep == 0 else upper.at[1 - e, slot]
        return pltpu.make_async_remote_copy(
            src_ref=source,
            dst_ref=halo.at[sweep, kind - 1, slot, e],
            send_sem=send_sem.at[kind - 1, e],
            recv_sem=recv_sem.at[sweep, kind - 1, slot],
            device_id=neighbours[kind][e],
            device_id_type=MESH,
        )

    def send(sweep, slots=range(UPPER)):
        for kind in (SECOND, FIRST):
            after, before = exists[kind]
            for ways, here in (
                ((0, 1), jnp.logical_and(after, before)),
                ((0,), jnp.logical_not(before)),
                ((1,), jnp.logical_not(after)),
            ):
                @pl.when(here)
                def _():
                    for slot in slots:
                        for e in ways:
                            transfer(sweep, kind, e, slot).start()

    def wait_arrived(sweep, kind, slot):
        place = halo.at[sweep, kind - 1, slot]
        pltpu.make_async_copy(place, place, recv_sem.at[sweep, kind - 1, slot]).wait()

    def wait_sent():
        for kind in (FIRST, SECOND):
            for e in range(2):
                @pl.when(exists[kind][e])
                def _():
                    sent = halo.at[:, kind - 1, :, e]
                    pltpu.make_async_copy(sent, sent, send_sem.at[kind - 1, e]).wait()

    barrier = pltpu.get_barrier_semaphore()
    arrivals = 0
    for kind in (SECOND, FIRST):
        for e in range(2):
            @pl.when(exists[kind][e])
            def _():
                pl.semaphore_signal(
                    barrier, inc=1, device_id=neighbours[kind][e], device_id_type=MESH
                )
            arrivals = arrivals + exists[kind][e].astype(jnp.int32)
    load = pltpu.make_async_copy(matrix_ref, held, load_sem)
    load.start()
    tables = [
        pltpu.make_async_copy(source, target, table_sem.at[index])
        for index, (source, target) in enumerate(
            [
                (left_hbm, left_ref), (rows_hbm, rows_ref), (slots_hbm, slots_ref),
                (counts_hbm, counts_ref), (diag_hbm, diag_ref),
            ]
        )
    ]
    for table in tables:
        table.start()
    pl.semaphore_wait(barrier, arrivals)
    load.wait()

    send(0)

    for kind in (FIRST, SECOND):
        for e in range(2):
            @pl.when(jnp.logical_not(exists[kind][1 - e]))
            def _():
                for sweep in range(2):
                    for slot in range(UPPER):
                        pltpu.make_async_copy(
                            matrix_ref.at[0, LOWER + slot],
                            halo.at[sweep, kind - 1, slot, e],
                            recv_sem.at[sweep, kind - 1, slot],
                        ).start()

    for table in tables:
        table.wait()

    def place_of(row):
        shift = lax.shift_right_arithmetic(row, 1) - own_domain
        own = shift == 0
        kind = jnp.where(own, OWN, jnp.where(jnp.abs(shift) == cols, FIRST, SECOND))
        e = jnp.where(own, lax.bitwise_and(row, 1), jnp.where(shift < 0, 0, 1))
        return kind, e

    @pl.loop(0, ROWS * SLOTS)
    def _(target):
        row, slot = lax.div(target, SLOTS), lax.rem(target, SLOTS)
        count = counts_ref[row, slot]
        for pair in range(PAIRS):
            kind, e = place_of(rows_ref[row, pair, slot])
            window = (kind * UPPER + slots_ref[row, pair, slot]) * 2 + e
            place = window * LEFTS + row * LOWER + left_ref[row, pair, slot]
            places[target * PAIRS + pair] = jnp.where(pair < count, place, WINDOW * LEFTS)

    @pl.loop(0, LEFTS)
    def _(target):
        kind, e = place_of(diag_ref[lax.div(target, LOWER), lax.rem(target, LOWER)])
        diag_places[target] = kind * 2 + e

    products[WINDOW * LEFTS] = jnp.zeros((BLOCK, BLOCK), F32)

    @pl.loop(0, LEFTS)
    def _(index):
        lower[pl.ds(pl.multiple_of(index * BLOCK, BLOCK), BLOCK)] = as_left(
            held[lax.div(index, LOWER), lax.rem(index, LOWER)]
        )

    def prepare(kind, slot, first, second):
        rights[kind * UPPER + slot] = jnp.concatenate([as_right(first), as_right(second)], axis=1)

    def multiply(kind, slot):
        group = kind * UPPER + slot
        both = product(lower[...], rights[group]).reshape(LEFTS, BLOCK, 2 * BLOCK)
        start = group * 2 * LEFTS
        products[pl.ds(start, LEFTS)] = both[:, :, :BLOCK]
        products[pl.ds(start + LEFTS, LEFTS)] = both[:, :, BLOCK:]

    def arrive(sweep, *steps):
        for kind, slot in steps:
            wait_arrived(sweep, kind, slot)
        for kind, slot in steps:
            prepare(kind, slot, halo[sweep, kind - 1, slot, 0], halo[sweep, kind - 1, slot, 1])

    def own(sweep, row, slot):
        return held[row, LOWER + slot] if sweep == 0 else upper[row, slot]

    def invert(sweep, *kinds):
        squares = []
        for kind in kinds:
            if kind == OWN:
                squares += [own(sweep, row, 0) for row in range(ROWS)]
            else:
                squares += [halo[sweep, kind - 1, 0, e] for e in range(2)]
        for index, inverse in enumerate(newton_inverses(squares)):
            inverses[kinds[0] * 2 + index] = as_right(inverse)

    def fill(sweep):
        for slot in range(UPPER):
            prepare(OWN, slot, own(sweep, 0, slot), own(sweep, 1, slot))
        for slot in range(UPPER):
            multiply(OWN, slot)
        invert(sweep, OWN)
        arrive(sweep, (FIRST, 0), (SECOND, 0))
        multiply(FIRST, 0)
        multiply(SECOND, 0)
        invert(sweep, FIRST, SECOND)
        arrive(sweep, (FIRST, 1), (SECOND, 1))
        multiply(FIRST, 1)
        multiply(SECOND, 1)
        arrive(sweep, (FIRST, 2), (SECOND, 2))
        multiply(FIRST, 2)
        multiply(SECOND, 2)
        arrive(sweep, (FIRST, 3), (SECOND, 3))
        multiply(FIRST, 3)
        multiply(SECOND, 3)

    def residue(row, slot):
        target = (row * SLOTS + slot) * PAIRS
        terms = [products[places[target + pair]] for pair in range(PAIRS)]
        return held[row, slot] - ((terms[0] + terms[1]) + (terms[2] + terms[3]))

    def lower_block(index):
        row, slot = index // LOWER, index % LOWER
        return product(as_left(residue(row, slot)), inverses[diag_places[index]])

    fill(0)
    for slots in ((0,), (1, 2, 3)):
        for slot in slots:
            for row in range(ROWS):
                upper[row, slot] = residue(row, LOWER + slot)
        send(1, slots)
    for index in range(LEFTS):
        lower[pl.ds(index * BLOCK, BLOCK)] = as_left(lower_block(index))

    fill(1)
    for index in range(LEFTS):
        out_ref[index // LOWER, index % LOWER] = lower_block(index)
    for slot in range(UPPER):
        for row in range(ROWS):
            out_ref[row, LOWER + slot] = residue(row, LOWER + slot)
    wait_sent()


def local(matrix, left_slots, right_rows, right_slots, pair_counts, diag_rows):
    operands = [matrix]
    operands += [jnp.swapaxes(table, 1, 2) for table in (left_slots, right_rows, right_slots)]
    operands += [pair_counts, diag_rows]
    return pl.pallas_call(
        kernel,
        out_shape=pltpu.VMEM(matrix.shape, F32),
        in_specs=[pl.BlockSpec(memory_space=pltpu.HBM)] * 6,
        out_specs=pl.BlockSpec(memory_space=pltpu.VMEM),
        scratch_shapes=[
            pltpu.SMEM((ROWS, PAIRS, SLOTS), jnp.int32),
            pltpu.SMEM((ROWS, PAIRS, SLOTS), jnp.int32),
            pltpu.SMEM((ROWS, PAIRS, SLOTS), jnp.int32),
            pltpu.SMEM((ROWS, SLOTS), jnp.int32),
            pltpu.SMEM((ROWS, LOWER), jnp.int32),
            pltpu.VMEM((ROWS, SLOTS, BLOCK, BLOCK), F32),
            pltpu.VMEM((LEFTS * BLOCK, 3 * BLOCK), BF16),
            pltpu.VMEM((3 * UPPER, 3 * BLOCK, 2 * BLOCK), BF16),
            pltpu.VMEM((ROWS, UPPER, BLOCK, BLOCK), F32),
            pltpu.VMEM((2, 2, UPPER, 2, BLOCK, BLOCK), F32),
            pltpu.VMEM((WINDOW * LEFTS + 1, BLOCK, BLOCK), F32),
            pltpu.VMEM((6, 3 * BLOCK, BLOCK), BF16),
            pltpu.SMEM((ROWS * SLOTS * PAIRS,), jnp.int32),
            pltpu.SMEM((LEFTS,), jnp.int32),
            pltpu.SemaphoreType.DMA,
            pltpu.SemaphoreType.DMA((5,)),
            pltpu.SemaphoreType.DMA((2, 2)),
            pltpu.SemaphoreType.DMA((2, 2, UPPER)),
        ],
        compiler_params=pltpu.CompilerParams(
            collective_id=0, has_side_effects=True, vmem_limit_bytes=48 * 2**20
        ),
    )(*(pltpu.with_memory_space_constraint(operand, pltpu.HBM) for operand in operands))


def solution(mesh):
    split_rows = ("dom", "col")
    return jax.shard_map(
        local,
        mesh=mesh,
        in_specs=(
            P(split_rows, None, None, None),
            P(split_rows, None, None),
            P(split_rows, None, None),
            P(split_rows, None, None),
            P(split_rows, None),
            P(split_rows, None),
        ),
        out_specs=P(split_rows, None, None, None),
        check_vma=False,
    )
```

```python
import functools

import jax
import jax.numpy as jnp
from jax import lax
from jax.experimental import pallas as pl
from jax.experimental.pallas import tpu as pltpu
from jax.sharding import PartitionSpec as P

LOWER = 4
UPPER = 4
SLOTS = 8
PAIRS = 4
ROWS = 2
BLOCK = 128
NEWTON_STEPS = 4
OWN, FIRST, SECOND = 0, 1, 2
WINDOW = 3 * UPPER * 2
LEFTS = ROWS * LOWER
MESH = pl.DeviceIdType.MESH
F32, BF16 = jnp.float32, jnp.bfloat16


def split(value):
    high = value.astype(BF16)
    return high, (value - high.astype(F32)).astype(BF16)


def as_left(value):
    high, low = split(value)
    return jnp.concatenate([high, low, high], axis=1)


def as_right(value):
    high, low = split(value)
    return jnp.concatenate([high, high, low], axis=0)


def product(left, right):
    return jnp.dot(left, right, preferred_element_type=F32)


def newton_inverses(squares):
    rows = lax.broadcasted_iota(jnp.int32, (BLOCK, BLOCK), 0)
    columns = lax.broadcasted_iota(jnp.int32, (BLOCK, BLOCK), 1)
    on_diagonal = rows == columns
    identity = jnp.where(on_diagonal, 1.0, 0.0).astype(F32)
    errors, approxes = [], []
    for square in squares:
        diagonal = jnp.where(on_diagonal, square, 0.0)
        error = identity - square * (1.0 / jnp.sum(diagonal, axis=0, keepdims=True))
        errors.append(error)
        approxes.append((identity + error) * (1.0 / jnp.sum(diagonal, axis=1, keepdims=True)))
    errors = [product(as_left(error), as_right(error)) for error in errors]
    for step in range(1, NEWTON_STEPS):
        for index, (error, approx) in enumerate(zip(errors, approxes)):
            right = as_right(error)
            if step < NEWTON_STEPS - 1:
                both = product(as_left(jnp.concatenate([approx, error], axis=0)), right)
                approxes[index] = approx + both[:BLOCK]
                errors[index] = both[BLOCK:]
            else:
                approxes[index] = approx + product(as_left(approx), right)
    return approxes


def kernel(
    matrix_ref, left_hbm, rows_hbm, slots_hbm, counts_hbm, diag_hbm, out_ref,
    left_ref, rows_ref, slots_ref, counts_ref, diag_ref,
    held, lower, rights, upper, halo, products, inverses, places, diag_places,
    load_sem, table_sem, send_sem, recv_sem,
):
    dom, col = lax.axis_index("dom"), lax.axis_index("col")
    doms, cols = lax.axis_size("dom"), lax.axis_size("col")
    own_domain = dom * cols + col
    neighbours = {FIRST: [(dom + 1, col), (dom - 1, col)], SECOND: [(dom, col + 1), (dom, col - 1)]}
    exists = {FIRST: [dom < doms - 1, dom > 0], SECOND: [col < cols - 1, col > 0]}

    def transfer(sweep, kind, e, slot):
        source = held.at[1 - e, LOWER + slot] if sweep == 0 else upper.at[1 - e, slot]
        return pltpu.make_async_remote_copy(
            src_ref=source,
            dst_ref=halo.at[sweep, kind - 1, slot, e],
            send_sem=send_sem.at[kind - 1, e],
            recv_sem=recv_sem.at[sweep, kind - 1, slot],
            device_id=neighbours[kind][e],
            device_id_type=MESH,
        )

    inside = functools.reduce(jnp.logical_and, exists[FIRST] + exists[SECOND])

    def send(sweep, slots=range(UPPER)):
        def start(kind, ways):
            for slot in slots:
                for e in ways:
                    transfer(sweep, kind, e, slot).start()

        @pl.when(inside)
        def _():
            for kind in (SECOND, FIRST):
                start(kind, (0, 1))

        @pl.when(jnp.logical_not(inside))
        def _():
            for kind in (SECOND, FIRST):
                after, before = exists[kind]
                for ways, here in (
                    ((0, 1), jnp.logical_and(after, before)),
                    ((0,), jnp.logical_not(before)),
                    ((1,), jnp.logical_not(after)),
                ):
                    pl.when(here)(functools.partial(start, kind, ways))

    def wait_arrived(sweep, kind, slot):
        place = halo.at[sweep, kind - 1, slot]
        pltpu.make_async_copy(place, place, recv_sem.at[sweep, kind - 1, slot]).wait()

    def wait_sent():
        for kind in (FIRST, SECOND):
            for e in range(2):
                @pl.when(exists[kind][e])
                def _():
                    sent = halo.at[:, kind - 1, :, e]
                    pltpu.make_async_copy(sent, sent, send_sem.at[kind - 1, e]).wait()

    barrier = pltpu.get_barrier_semaphore()
    arrivals = 0
    for kind in (SECOND, FIRST):
        for e in range(2):
            @pl.when(exists[kind][e])
            def _():
                pl.semaphore_signal(
                    barrier, inc=1, device_id=neighbours[kind][e], device_id_type=MESH
                )
            arrivals = arrivals + exists[kind][e].astype(jnp.int32)
    load = pltpu.make_async_copy(matrix_ref, held, load_sem)
    load.start()
    tables = [
        pltpu.make_async_copy(source, target, table_sem.at[index])
        for index, (source, target) in enumerate(
            [
                (left_hbm, left_ref), (rows_hbm, rows_ref), (slots_hbm, slots_ref),
                (counts_hbm, counts_ref), (diag_hbm, diag_ref),
            ]
        )
    ]
    for table in tables:
        table.start()
    pl.semaphore_wait(barrier, arrivals)
    load.wait()

    send(0)

    for kind in (FIRST, SECOND):
        for e in range(2):
            @pl.when(jnp.logical_not(exists[kind][1 - e]))
            def _():
                for sweep in range(2):
                    for slot in range(UPPER):
                        pltpu.make_async_copy(
                            matrix_ref.at[0, LOWER + slot],
                            halo.at[sweep, kind - 1, slot, e],
                            recv_sem.at[sweep, kind - 1, slot],
                        ).start()

    for table in tables:
        table.wait()

    def place_of(row):
        shift = lax.shift_right_arithmetic(row, 1) - own_domain
        own = shift == 0
        kind = jnp.where(own, OWN, jnp.where(jnp.abs(shift) == cols, FIRST, SECOND))
        e = jnp.where(own, lax.bitwise_and(row, 1), jnp.where(shift < 0, 0, 1))
        return kind, e

    @pl.loop(0, ROWS * SLOTS)
    def _(target):
        row, slot = lax.div(target, SLOTS), lax.rem(target, SLOTS)
        count = counts_ref[row, slot]
        for pair in range(PAIRS):
            kind, e = place_of(rows_ref[row, pair, slot])
            window = (kind * UPPER + slots_ref[row, pair, slot]) * 2 + e
            place = window * LEFTS + row * LOWER + left_ref[row, pair, slot]
            places[target * PAIRS + pair] = jnp.where(pair < count, place, WINDOW * LEFTS)

    @pl.loop(0, LEFTS)
    def _(target):
        kind, e = place_of(diag_ref[lax.div(target, LOWER), lax.rem(target, LOWER)])
        diag_places[target] = kind * 2 + e

    products[WINDOW * LEFTS] = jnp.zeros((BLOCK, BLOCK), F32)

    @pl.loop(0, LEFTS)
    def _(index):
        lower[pl.ds(pl.multiple_of(index * BLOCK, BLOCK), BLOCK)] = as_left(
            held[lax.div(index, LOWER), lax.rem(index, LOWER)]
        )

    def prepare(kind, slot, first, second):
        rights[kind * UPPER + slot] = jnp.concatenate([as_right(first), as_right(second)], axis=1)

    def multiply(kind, slot):
        group = kind * UPPER + slot
        both = product(lower[...], rights[group]).reshape(LEFTS, BLOCK, 2 * BLOCK)
        start = group * 2 * LEFTS
        products[pl.ds(start, LEFTS)] = both[:, :, :BLOCK]
        products[pl.ds(start + LEFTS, LEFTS)] = both[:, :, BLOCK:]

    def arrive(sweep, *steps):
        for kind, slot in steps:
            wait_arrived(sweep, kind, slot)
        for kind, slot in steps:
            prepare(kind, slot, halo[sweep, kind - 1, slot, 0], halo[sweep, kind - 1, slot, 1])

    def own(sweep, row, slot):
        return held[row, LOWER + slot] if sweep == 0 else upper[row, slot]

    def invert(sweep, *kinds):
        squares = []
        for kind in kinds:
            if kind == OWN:
                squares += [own(sweep, row, 0) for row in range(ROWS)]
            else:
                squares += [halo[sweep, kind - 1, 0, e] for e in range(2)]
        for index, inverse in enumerate(newton_inverses(squares)):
            inverses[kinds[0] * 2 + index] = as_right(inverse)

    def fill(sweep):
        for slot in range(UPPER):
            prepare(OWN, slot, own(sweep, 0, slot), own(sweep, 1, slot))
        for slot in range(UPPER):
            multiply(OWN, slot)
        invert(sweep, OWN)
        arrive(sweep, (FIRST, 0), (SECOND, 0))
        multiply(FIRST, 0)
        multiply(SECOND, 0)
        invert(sweep, FIRST, SECOND)
        arrive(sweep, (FIRST, 1), (SECOND, 1))
        multiply(FIRST, 1)
        multiply(SECOND, 1)
        arrive(sweep, (FIRST, 2), (SECOND, 2))
        multiply(FIRST, 2)
        multiply(SECOND, 2)
        arrive(sweep, (FIRST, 3), (SECOND, 3))
        multiply(FIRST, 3)
        multiply(SECOND, 3)

    def residue(row, slot):
        target = (row * SLOTS + slot) * PAIRS
        terms = [products[places[target + pair]] for pair in range(PAIRS)]
        return held[row, slot] - ((terms[0] + terms[1]) + (terms[2] + terms[3]))

    def lower_block(index):
        row, slot = index // LOWER, index % LOWER
        return product(as_left(residue(row, slot)), inverses[diag_places[index]])

    fill(0)
    for slot in range(UPPER):
        for row in range(ROWS):
            upper[row, slot] = residue(row, LOWER + slot)
    send(1)
    for index in range(LEFTS):
        lower[pl.ds(index * BLOCK, BLOCK)] = as_left(lower_block(index))

    fill(1)
    for index in range(LEFTS):
        out_ref[index // LOWER, index % LOWER] = lower_block(index)
    for slot in range(UPPER):
        for row in range(ROWS):
            out_ref[row, LOWER + slot] = residue(row, LOWER + slot)
    wait_sent()


def local(matrix, left_slots, right_rows, right_slots, pair_counts, diag_rows):
    operands = [matrix]
    operands += [jnp.swapaxes(table, 1, 2) for table in (left_slots, right_rows, right_slots)]
    operands += [pair_counts, diag_rows]
    return pl.pallas_call(
        kernel,
        out_shape=pltpu.VMEM(matrix.shape, F32),
        in_specs=[pl.BlockSpec(memory_space=pltpu.HBM)] * 6,
        out_specs=pl.BlockSpec(memory_space=pltpu.VMEM),
        scratch_shapes=[
            pltpu.SMEM((ROWS, PAIRS, SLOTS), jnp.int32),
            pltpu.SMEM((ROWS, PAIRS, SLOTS), jnp.int32),
            pltpu.SMEM((ROWS, PAIRS, SLOTS), jnp.int32),
            pltpu.SMEM((ROWS, SLOTS), jnp.int32),
            pltpu.SMEM((ROWS, LOWER), jnp.int32),
            pltpu.VMEM((ROWS, SLOTS, BLOCK, BLOCK), F32),
            pltpu.VMEM((LEFTS * BLOCK, 3 * BLOCK), BF16),
            pltpu.VMEM((3 * UPPER, 3 * BLOCK, 2 * BLOCK), BF16),
            pltpu.VMEM((ROWS, UPPER, BLOCK, BLOCK), F32),
            pltpu.VMEM((2, 2, UPPER, 2, BLOCK, BLOCK), F32),
            pltpu.VMEM((WINDOW * LEFTS + 1, BLOCK, BLOCK), F32),
            pltpu.VMEM((6, 3 * BLOCK, BLOCK), BF16),
            pltpu.SMEM((ROWS * SLOTS * PAIRS,), jnp.int32),
            pltpu.SMEM((LEFTS,), jnp.int32),
            pltpu.SemaphoreType.DMA,
            pltpu.SemaphoreType.DMA((5,)),
            pltpu.SemaphoreType.DMA((2, 2)),
            pltpu.SemaphoreType.DMA((2, 2, UPPER)),
        ],
        compiler_params=pltpu.CompilerParams(
            collective_id=0, has_side_effects=True, vmem_limit_bytes=48 * 2**20
        ),
    )(*(pltpu.with_memory_space_constraint(operand, pltpu.HBM) for operand in operands))


def solution(mesh):
    split_rows = ("dom", "col")
    return jax.shard_map(
        local,
        mesh=mesh,
        in_specs=(
            P(split_rows, None, None, None),
            P(split_rows, None, None),
            P(split_rows, None, None),
            P(split_rows, None, None),
            P(split_rows, None),
            P(split_rows, None),
        ),
        out_specs=P(split_rows, None, None, None),
        check_vma=False,
    )
```
